256 devices in a mesh: clus: 2 (over core), aux: 128 (over x, z, y).
Axes of the slice: x: 4, y: 4, z: 8, core: 2. Of those that a mesh axis runs over, the one named last changes fastest.
Arguments:
- density3: bfloat16 [2, 2048, 48, 768], P('clus', 'aux'), may hold values from -6 to 6
- fitted_ints: bfloat16 [2, 2048, 48, 768], P('clus', 'aux'), may hold values from -0.03125 to 0.03125
- virt_coeffs: bfloat16 [2, 1024, 768], P('clus'), may hold values from -0.21875 to 0.21875
- dom_list: int32 [2, 2048], P('clus'), may hold values from 0 to 2559, as said below
Outputs:
- half_density: bfloat16 [2, 2048, 48, 1024], P('clus', 'aux')
- metric_density: float32 [2560, 2560], P('aux', 'clus')
The draws below stay inside these ranges and needn't reach their ends.
Inputs may be any that keep to these rules, and one draw needn't show every extreme that they name: `dom_list`: each row names 2048 different global auxiliary functions.
All inputs are finite; a program needn't handle non-finite values.
Results may differ from the reference program's by a relative error of at most 0.001.
Values may be sent and summed in bfloat16 or wider, within the bound.
A program may use at most 192 MiB of HBM per device.

```python
import jax
import jax.numpy as jnp

NO = 48
NV = 768
NAO = 1024
DOM = 2048
NAUXG = 2560


def draw_dom_list(key, part):
    key = jax.random.fold_in(key, 7)
    listed = []
    for cluster in range(2):
        first_key, second_key = jax.random.split(jax.random.fold_in(key, cluster))
        others = jax.random.permutation(first_key, NAUXG - 1)[:DOM - 1].astype(jnp.int32)
        picked = jnp.concatenate([jnp.full((1,), NAUXG - 1, jnp.int32), others])
        listed.append(jax.random.permutation(second_key, picked).astype(jnp.int32))
    return jnp.stack(listed)


def levels(rng, extent, pieces, low, largest):
    factor_of = 1.0
    for dim, shards_of in pieces:
        heights = jax.random.uniform(jax.random.fold_in(jax.random.fold_in(rng, 6), dim), (shards_of,), jnp.float32, low / len(pieces), largest / len(pieces))
        factor_of = factor_of * jnp.repeat(jnp.exp(heights), extent[dim] // shards_of).reshape((-1,) + (1,) * (len(extent) - 1 - dim))
    return factor_of


def bell_draw(stream_key, shape, deviation, limit, cuts=(), kind=jnp.bfloat16):
    factor_of = levels(stream_key, shape, cuts, -0.22, 0.18) if cuts else 1.0
    array = jax.random.normal(stream_key, shape, jnp.float32) * deviation * factor_of
    return jnp.minimum(jnp.maximum(array, -limit), limit).astype(kind)


def setup_inputs(seed: int = 0) -> dict:
    seeds = jax.random.split(jax.random.key(seed), 5)
    return {
        "density3": bell_draw(seeds[0], (2, DOM, NO, NV), 1.0, 6.0, ((0, 2), (1, 128))),
        "fitted_ints": bell_draw(seeds[1], (2, DOM, NO, NV), (NO * NV) ** -0.5, 0.03125, ((0, 2), (1, 128))),
        "virt_coeffs": bell_draw(seeds[2], (2, NAO, NV), NV ** -0.5, 0.21875, ((0, 2),)),
        "dom_list": draw_dom_list(jax.random.fold_in(seeds[4], 71), 0),
    }


def reference(density3, fitted_ints, virt_coeffs, dom_list):
    halves = []
    metric = jnp.zeros((NAUXG, NAUXG), jnp.float32)
    for cluster in range(2):
        flat_dens = density3[cluster].reshape(DOM * NO, NV)
        back = jnp.dot(flat_dens, virt_coeffs[cluster].T, preferred_element_type=jnp.float32)
        halves.append(back.astype(jnp.bfloat16).reshape(DOM, NO, NAO))
        left = density3[cluster].reshape(DOM, NO * NV)
        right = fitted_ints[cluster].reshape(DOM, NO * NV)
        local_metric = jnp.dot(left, right.T, preferred_element_type=jnp.float32)
        index = dom_list[cluster].astype(jnp.int32)
        metric = metric.at[index[:, None], index[None, :]].add(local_metric)
    return jnp.stack(halves), metric
```

```python
import jax
import jax.numpy as jnp
from jax import lax
from jax.experimental import pallas as pl
from jax.experimental.pallas import tpu as pltpu
from jax.sharding import PartitionSpec as P

MESH = pl.DeviceIdType.MESH
X, Y, Z = 4, 4, 8
ROWS = 16
NO, NV = 48, 768
CH = NO // Z
GP = Z * ROWS
BLK = X * GP
DOM = X * Y * Z * ROWS
SLAB = 20
HALF = 1280
ZB = BLK // Z
QH = ZB // 2
GW = Z * Y * 32
ZORDER = (4, 3, 5, 2, 6, 1, 7)
NT = (((1,), (1,)), ((), ()))


def split(v):
    hi = v.astype(jnp.bfloat16)
    lo = (v - hi.astype(jnp.float32)).astype(jnp.bfloat16)
    return hi, lo


def kernel(dens, fit, dom_ref, out_ref,
           stage, sent, gath, acc, ring, spread, wide, moved, turned, last, doms, onep, oneq,
           load_sem, a2a_sem, gat_sem, ring_sem, misc_sem, a2a_send, gat_send, ring_send, misc_send):
    c = lax.axis_index("clus")
    aux = lax.axis_index("aux")
    y = lax.rem(aux, Y)
    z = lax.rem(aux // Y, Z)
    x = aux // (Y * Z)

    def dev(dx, dy, dz, core=c):
        xx, yy, zz = lax.rem(x + dx, X), lax.rem(y + dy, Y), lax.rem(z + dz, Z)
        return (core, (xx * Z + zz) * Y + yy)

    def remote(src, dst, send, recv, where):
        return pltpu.make_async_remote_copy(
            src_ref=src, dst_ref=dst, send_sem=send, recv_sem=recv,
            device_id=where, device_id_type=MESH)

    def arrived(like, sem):
        pltpu.make_async_copy(like, like, sem).wait()

    loads = []
    for group in range(3):
        for arr, ref in ((0, dens), (1, fit)):
            load = pltpu.make_async_copy(
                ref.at[:, pl.ds(16 * group, 16), :], stage.at[arr, group], load_sem.at[arr, group])
            load.start()
            loads.append(load)

    barrier = pltpu.get_barrier_semaphore()
    peers = [dev(0, 0, d) for d in range(1, Z)] + [dev(d, 0, 0) for d in range(1, X)]
    for core in (c, 1 - c):
        peers += [dev(0, d, 0, core) for d in range(1, Y)]
    peers.append(dev(0, 0, 0, 1 - c))
    for peer in peers:
        pl.semaphore_signal(barrier, inc=1, device_id=peer, device_id_type=MESH)

    def relayout(group):
        for arr in range(2):
            loads[2 * group + arr].wait()
            block = stage[arr, group].astype(jnp.float32)
            sent[arr, pl.ds(16 * group, 16)] = jnp.swapaxes(block, 0, 1).astype(jnp.bfloat16)

    def slot(arr):
        return y if arr == 0 else x

    def scatter(chunk):
        for arr in range(2):
            base = pl.multiple_of(slot(arr) * GP + z * ROWS, ROWS)
            target = gath.at[arr, chunk, pl.ds(base, ROWS), :]
            pltpu.make_async_copy(sent.at[arr, Z * chunk + z], target, a2a_sem.at[arr, chunk]).start()
            for d in ZORDER:
                other = lax.rem(z + d, Z)
                remote(sent.at[arr, Z * chunk + other], target,
                       a2a_send.at[arr], a2a_sem.at[arr, chunk], dev(0, 0, d)).start()

    def gather(chunk):
        for arr in range(2):
            arrived(sent.at[arr, pl.ds(0, Z)], a2a_sem.at[arr, chunk])
            base = pl.multiple_of(slot(arr) * GP, GP)
            part = gath.at[arr, chunk, pl.ds(base, GP), :]
            for d in (2, 1, 3):
                where = dev(0, d, 0) if arr == 0 else dev(d, 0, 0)
                remote(part, part, gat_send.at[arr], gat_sem.at[arr, chunk], where).start()

    def multiply(chunk):
        for arr in range(2):
            arrived(gath.at[arr, chunk, pl.ds(0, 3 * GP), :], gat_sem.at[arr, chunk])

        @pl.loop(0, 2)
        def _(half):
            rows = pl.ds(pl.multiple_of(half * (BLK // 2), BLK // 2), BLK // 2)
            prod = lax.dot_general(gath[1, chunk, rows, :], gath[0, chunk], NT,
                                   preferred_element_type=jnp.float32)
            if chunk == 0:
                acc[rows, :] = prod
            else:
                acc[rows, :] += prod

    def one_hot_rows():
        domp = dom_ref[0:1, :]

        @pl.loop(0, GW // 128)
        def _(b):
            row = lax.broadcasted_iota(jnp.int32, (128, DOM), 0) + b * 128
            pad = lax.rem(row, 32)
            goal = jnp.where(pad < SLAB, x * (Y * Z * SLAB) + (row // 32) * SLAB + pad, -1)
            onep[pl.ds(pl.multiple_of(b * 128, 128), 128), :] = jnp.where(
                goal == domp, 1.0, 0.0).astype(jnp.bfloat16)

    def one_hot_columns(cluster):
        domq = doms[cluster, 0:1, :]

        @pl.loop(0, HALF // 128)
        def _(b):
            goal = lax.broadcasted_iota(jnp.int32, (128, DOM), 0) + (c * HALF + b * 128)
            oneq[cluster, pl.ds(pl.multiple_of(b * 128, 128), 128), :] = jnp.where(
                goal == domq, 1.0, 0.0).astype(jnp.bfloat16)

    relayout(0)
    pl.semaphore_wait(barrier, len(peers))
    scatter(0)
    scatter(1)
    own_dom = pltpu.make_async_copy(dom_ref.at[pl.ds(8, 8)], doms.at[c], load_sem.at[0, 3])
    own_dom.start()
    remote_dom = remote(dom_ref.at[pl.ds(8, 8)], doms.at[c], misc_send.at[0], misc_sem.at[0], dev(0, 0, 0, 1 - c))
    remote_dom.start()
    relayout(1)
    relayout(2)
    for chunk in range(CH):
        gather(chunk)
        if chunk + 2 < CH:
            scatter(chunk + 2)
        if chunk == 1:
            one_hot_rows()
        if chunk == 2:
            own_dom.wait()
            remote_dom.wait()
            one_hot_columns(0)
        if chunk == 3:
            one_hot_columns(1)
        if chunk > 0:
            multiply(chunk - 1)
    multiply(CH - 1)

    def flow(direction, half):
        return 2 * direction + half

    def piece(direction, half, away):
        d = lax.rem(z + (Z - away if direction == 0 else away), Z)
        return pl.ds(pl.multiple_of(d * ZB + half * QH, QH), QH)

    def push(direction, half, step, src):
        f = flow(direction, half)
        remote(src, ring.at[f, step], ring_send.at[f, step], ring_sem.at[f, step],
               dev(0, 0, Z - 1 if direction == 0 else 1)).start()

    legs = ((0, 0, 4), (1, 1, 4), (0, 1, 3), (1, 0, 3))
    for direction, half, far in legs:
        push(direction, half, 0, acc.at[piece(direction, half, far)])
    for step in range(3):
        for direction, half, far in legs:
            if step < far - 1:
                f = flow(direction, half)
                arrived(ring.at[f, step], ring_sem.at[f, step])
                ring[f, step] += acc[piece(direction, half, far - 1 - step), :]
                push(direction, half, step + 1, ring.at[f, step])
    for direction, half, far in legs:
        f = flow(direction, half)
        arrived(ring.at[f, far - 1], ring_sem.at[f, far - 1])
    for half in range(2):
        mine = acc[piece(0, half, 0), :]
        for direction in range(2):
            far = 4 if direction == half else 3
            mine = mine + ring[flow(direction, half), far - 1]
        hi, lo = split(mine)
        spread[x, pl.ds(half * QH, QH), :] = hi
        spread[x, pl.ds(ZB + half * QH, QH), :] = lo

    for d in (2, 1, 3):
        remote(spread.at[x], spread.at[x], misc_send.at[1], misc_sem.at[1], dev(d, 0, 0)).start()
    arrived(spread.at[pl.ds(0, 3)], misc_sem.at[1])
    both = None
    for k in range(X):
        term = lax.dot_general(spread[k], onep[:, k * BLK:(k + 1) * BLK], NT,
                               preferred_element_type=jnp.float32)
        both = term if both is None else both + term
    full = both[:ZB] + both[ZB:]
    for k in range(Z):
        wide[k] = full[:, 128 * k:128 * (k + 1)]

    for d in ZORDER:
        remote(wide.at[lax.rem(z + d, Z)], moved.at[z], misc_send.at[2], misc_sem.at[2], dev(0, 0, d)).start()
    moved[z] = wide[z]
    arrived(wide.at[pl.ds(0, Z - 1)], misc_sem.at[2])
    flat = moved[...].reshape(BLK, 128).T
    for k in range(Y):
        turned[k] = flat[32 * k:32 * k + 24]
    for core in (c, 1 - c):
        for d in (2, 1, 3):
            remote(turned.at[lax.rem(y + d, Y)], last.at[c * Y + y], misc_send.at[3], misc_sem.at[3],
                   dev(0, d, 0, core)).start()
    remote(turned.at[y], last.at[c * Y + y], misc_send.at[3], misc_sem.at[3], dev(0, 0, 0, 1 - c)).start()
    last[c * Y + y] = turned[y]
    arrived(last.at[pl.ds(0, 2 * Y - 1)], misc_sem.at[3])

    total = None
    for cluster in range(2):
        for k in range(Y):
            hi, lo = split(last[cluster * Y + k])
            cols = oneq[cluster, :, k * BLK:(k + 1) * BLK]
            for part in (hi, lo):
                term = lax.dot_general(part, cols, NT, preferred_element_type=jnp.float32)
                total = term if total is None else total + term
    out_ref[...] = total[:SLAB]

    for arr in range(2):
        arrived(sent.at[arr, pl.ds(0, CH * (Z - 1))], a2a_send.at[arr])
        arrived(gath.at[arr, :, pl.ds(0, 3 * GP), :], gat_send.at[arr])
    for direction, half, far in legs:
        f = flow(direction, half)
        for step in range(far):
            arrived(ring.at[f, step], ring_send.at[f, step])
    arrived(spread.at[pl.ds(0, 3)], misc_send.at[1])
    arrived(wide.at[pl.ds(0, Z - 1)], misc_send.at[2])
    arrived(last.at[pl.ds(0, 2 * Y - 1)], misc_send.at[3])


def shards(density3, fitted_ints, virt_coeffs, dom_list):
    flat = density3[0].reshape(ROWS * NO, NV)
    back = lax.dot_general(flat, virt_coeffs[0], NT, preferred_element_type=jnp.float32)
    half_density = back.astype(jnp.bfloat16).reshape(1, ROWS, NO, virt_coeffs.shape[1])
    dom = dom_list[0].reshape(X, Z, Y, ROWS)
    domp = jnp.broadcast_to(dom.transpose(0, 2, 1, 3).reshape(1, DOM), (8, DOM))
    domq = jnp.broadcast_to(dom.transpose(2, 0, 1, 3).reshape(1, DOM), (8, DOM))
    orders = jnp.concatenate([domp, domq], axis=0)
    dma = pltpu.SemaphoreType.DMA
    metric = pl.pallas_call(
        kernel,
        out_shape=jax.ShapeDtypeStruct((SLAB, HALF), jnp.float32),
        in_specs=[pl.BlockSpec(memory_space=pl.ANY), pl.BlockSpec(memory_space=pl.ANY),
                  pl.BlockSpec(memory_space=pltpu.VMEM)],
        out_specs=pl.BlockSpec(memory_space=pltpu.VMEM),
        scratch_shapes=[
            pltpu.VMEM((2, 3, ROWS, 16, NV), jnp.bfloat16),
            pltpu.VMEM((2, NO, ROWS, NV), jnp.bfloat16),
            pltpu.VMEM((2, CH, BLK, NV), jnp.bfloat16),
            pltpu.VMEM((BLK, BLK), jnp.float32),
            pltpu.VMEM((4, 4, QH, BLK), jnp.float32),
            pltpu.VMEM((X, 2 * ZB, BLK), jnp.bfloat16),
            pltpu.VMEM((Z, ZB, 128), jnp.float32),
            pltpu.VMEM((Z, ZB, 128), jnp.float32),
            pltpu.VMEM((Y, 24, BLK), jnp.float32),
            pltpu.VMEM((2 * Y, 24, BLK), jnp.float32),
            pltpu.VMEM((2, 8, DOM), jnp.int32),
            pltpu.VMEM((GW, DOM), jnp.bfloat16),
            pltpu.VMEM((2, HALF, DOM), jnp.bfloat16),
            dma((2, 4)), dma((2, CH)), dma((2, CH)), dma((4, 4)), dma((4,)),
            dma((2,)), dma((2,)), dma((4, 4)), dma((4,)),
        ],
        compiler_params=pltpu.CompilerParams(
            collective_id=0, has_side_effects=True, vmem_limit_bytes=56 * 2**20),
    )(density3[0], fitted_ints[0], orders)
    return (half_density, metric)


def solution(mesh):
    in_specs = (
        P("clus", "aux", None, None),
        P("clus", "aux", None, None),
        P("clus", None, None),
        P("clus", None),
    )
    out_specs = (P("clus", "aux", None, None), P("aux", "clus"))
    return jax.shard_map(shards, mesh=mesh, in_specs=in_specs, out_specs=out_specs, check_vma=False)
```

```python
import jax
import jax.numpy as jnp
from jax import lax
from jax.experimental import pallas as pl
from jax.experimental.pallas import tpu as pltpu
from jax.sharding import PartitionSpec as P

MESH = pl.DeviceIdType.MESH
X, Y, Z = 4, 4, 8
ROWS = 16
NO, NV = 48, 768
CH = NO // Z
GP = Z * ROWS
BLK = X * GP
DOM = X * Y * Z * ROWS
SLAB = 20
HALF = 1280
HB = BLK // 2
ZH = HB // Z
QB = ZH // 2
PARTS = ((0, 0, 128), (0, 128, NV), (1, 0, NV), (2, 0, NV), (3, 0, NV), (4, 0, 512), (4, 512, NV),
         (5, 0, 256), (5, 256, 512), (5, 512, 640), (5, 640, NV))
RELAYED = 5
GW = Z * Y * 32
ZORDER = (4, 3, 5, 2, 6, 1, 7)
NT = (((1,), (1,)), ((), ()))


def split(v):
    hi = v.astype(jnp.bfloat16)
    lo = (v - hi.astype(jnp.float32)).astype(jnp.bfloat16)
    return hi, lo


def kernel(dens, fit, dom_ref, out_ref,
           stage, sent, gath, acc, ring, spread, wide, moved, turned, last, doms, onep, oneq,
           load_sem, a2a_sem, near_sem, gat_sem, ring_sem, spread_sem, moved_sem, last_sem, misc_sem,
           a2a_send, gat_send, ring_send, spread_send, moved_send, last_send):
    c = lax.axis_index("clus")
    aux = lax.axis_index("aux")
    y = lax.rem(aux, Y)
    z = lax.rem(aux // Y, Z)
    x = aux // (Y * Z)

    def dev(dx, dy, dz, core=c):
        xx, yy, zz = lax.rem(x + dx, X), lax.rem(y + dy, Y), lax.rem(z + dz, Z)
        return (core, (xx * Z + zz) * Y + yy)

    def remote(src, dst, send, recv, where):
        return pltpu.make_async_remote_copy(
            src_ref=src, dst_ref=dst, send_sem=send, recv_sem=recv,
            device_id=where, device_id_type=MESH)

    def arrived(like, sem):
        pltpu.make_async_copy(like, like, sem).wait()

    loads = []
    for group in range(3):
        for arr, ref in ((0, dens), (1, fit)):
            load = pltpu.make_async_copy(
                ref.at[:, pl.ds(16 * group, 16), :], stage.at[arr, group], load_sem.at[arr, group])
            load.start()
            loads.append(load)

    barrier = pltpu.get_barrier_semaphore()
    peers = [dev(0, 0, d) for d in range(1, Z)] + [dev(d, 0, 0) for d in range(1, X)]
    for core in (c, 1 - c):
        peers += [dev(0, d, 0, core) for d in range(1, Y)]
    peers.append(dev(0, 0, 0, 1 - c))
    for peer in peers:
        pl.semaphore_signal(barrier, inc=1, device_id=peer, device_id_type=MESH)

    def relayout(group):
        for arr in range(2):
            loads[2 * group + arr].wait()
            block = stage[arr, group].astype(jnp.float32)
            sent[arr, pl.ds(16 * group, 16)] = jnp.swapaxes(block, 0, 1).astype(jnp.bfloat16)

    def slot(arr):
        return y if arr == 0 else x

    def scatter(n):
        chunk, low, high = PARTS[n]
        lanes = pl.ds(low, high - low)
        for arr in range(2):
            base = pl.multiple_of(slot(arr) * GP + z * ROWS, ROWS)
            target = gath.at[arr, chunk, pl.ds(base, ROWS), lanes]
            pltpu.make_async_copy(sent.at[arr, Z * chunk + z, :, lanes], target, a2a_sem.at[arr, n]).start()
            for d in ZORDER:
                other = lax.rem(z + d, Z)
                remote(sent.at[arr, Z * chunk + other, :, lanes], target,
                       a2a_send.at[arr], a2a_sem.at[arr, n], dev(0, 0, d)).start()

    def around(arr, d):
        return dev(0, d, 0) if arr == 0 else dev(d, 0, 0)

    def gather(n):
        chunk, low, high = PARTS[n]
        lanes = pl.ds(low, high - low)
        for arr in range(2):
            arrived(sent.at[arr, pl.ds(0, Z), :, lanes], a2a_sem.at[arr, n])
            base = pl.multiple_of(slot(arr) * GP, GP)
            part = gath.at[arr, chunk, pl.ds(base, GP), lanes]
            if n < RELAYED:
                for d in (1, 3):
                    remote(part, part, gat_send.at[arr], near_sem.at[arr, n, d // 2], around(arr, d)).start()
            else:
                for d in (2, 1, 3):
                    remote(part, part, gat_send.at[arr], gat_sem.at[arr, n], around(arr, d)).start()

    def relay(n):
        chunk, low, high = PARTS[n]
        lanes = pl.ds(low, high - low)
        for arr in range(2):
            for d in (1, 3):
                base = lax.rem(slot(arr) + 4 - d, 4) * GP
                arrived(gath.at[arr, chunk, pl.ds(0, GP), lanes], near_sem.at[arr, n, d // 2])
                rows = pl.ds(pl.multiple_of(base + (d // 2) * (GP // 2), GP // 2), GP // 2)
                part = gath.at[arr, chunk, rows, lanes]
                remote(part, part, gat_send.at[arr], gat_sem.at[arr, n], around(arr, d)).start()

    def multiply(n):
        chunk, low, high = PARTS[n]
        for arr in range(2):
            rest = GP if n < RELAYED else 3 * GP
            arrived(gath.at[arr, chunk, pl.ds(0, rest), pl.ds(low, high - low)], gat_sem.at[arr, n])

        @pl.loop(0, 2)
        def _(half):
            rows = pl.ds(pl.multiple_of(half * (BLK // 2), BLK // 2), BLK // 2)
            prod = lax.dot_general(gath[1, chunk, rows, low:high], gath[0, chunk, :, low:high], NT,
                                   preferred_element_type=jnp.float32)
            if n == 0:
                acc[rows, :] = prod
            else:
                acc[rows, :] += prod

    def order_list():
        rows = [dom_ref[0:1, k * BLK:(k + 1) * BLK] for k in range(X)]
        digits = jnp.concatenate([v // 64 for v in rows] + [lax.rem(v, 64) for v in rows], axis=0)
        digits = digits.astype(jnp.float32).astype(jnp.bfloat16)
        moved_to = None
        for k in range(Y):
            n = lax.broadcasted_iota(jnp.int32, (128, BLK), 0) + 128 * k
            m = lax.broadcasted_iota(jnp.int32, (128, BLK), 1)
            source = lax.rem(m // ROWS, Z) * (Y * ROWS) + (m // GP) * ROWS + lax.rem(m, ROWS)
            perm = jnp.where(n == source, 1.0, 0.0).astype(jnp.bfloat16)
            term = lax.dot_general(digits[:, 128 * k:128 * (k + 1)], perm, (((1,), (0,)), ((), ())),
                                   preferred_element_type=jnp.float32)
            moved_to = term if moved_to is None else moved_to + term
        listed = (moved_to[:X] * 64.0 + moved_to[X:]).astype(jnp.int32)
        doms[c] = jnp.concatenate([listed, listed], axis=0)

    def one_hot_rows():
        @pl.loop(0, GW // 128)
        def _(b):
            row = lax.broadcasted_iota(jnp.int32, (128, BLK), 0) + b * 128
            pad = lax.rem(row, 32)
            goal = jnp.where(pad < SLAB, x * (Y * Z * SLAB) + (row // 32) * SLAB + pad, -1)
            for k in range(X):
                onep[pl.ds(pl.multiple_of(b * 128, 128), 128), k * BLK:(k + 1) * BLK] = jnp.where(
                    goal == doms[c, k:k + 1, :], 1.0, 0.0).astype(jnp.bfloat16)

    def one_hot_columns(cluster):
        @pl.loop(0, HALF // 128)
        def _(b):
            goal = lax.broadcasted_iota(jnp.int32, (128, GP), 0) + (c * HALF + b * 128)
            for k in range(DOM // GP):
                high, col, low = k // (2 * Y), (k // 2) % Y, k % 2
                names = doms[cluster, 2 * high + low:2 * high + low + 1, col * GP:(col + 1) * GP]
                oneq[cluster, pl.ds(pl.multiple_of(b * 128, 128), 128), k * GP:(k + 1) * GP] = jnp.where(
                    goal == names, 1.0, 0.0).astype(jnp.bfloat16)

    relayout(0)
    pl.semaphore_wait(barrier, len(peers))
    scatter(0)
    scatter(1)
    relayout(1)
    order_list()
    remote_dom = remote(doms.at[c], doms.at[c], misc_sem.at[0], misc_sem.at[1], dev(0, 0, 0, 1 - c))
    remote_dom.start()
    gather(0)
    scatter(2)
    relayout(2)
    gather(1)
    scatter(3)
    relay(0)
    gather(2)
    scatter(4)
    one_hot_rows()
    relay(1)
    multiply(0)
    gather(3)
    scatter(5)
    scatter(6)
    remote_dom.wait()
    one_hot_columns(0)
    relay(2)
    multiply(1)
    gather(4)
    scatter(7)
    scatter(8)
    scatter(9)
    scatter(10)
    relay(3)
    multiply(2)
    one_hot_columns(1)
    gather(5)
    relay(4)
    multiply(3)
    gather(6)
    gather(7)
    multiply(4)
    gather(8)
    gather(9)
    gather(10)
    multiply(5)
    multiply(6)
    multiply(7)
    multiply(8)
    multiply(9)
    multiply(10)

    def rows_of(quarter, d):
        return pl.ds(pl.multiple_of((quarter // 2) * HB + d * ZH + (quarter % 2) * QB, QB), QB)

    def push(direction, quarter, step, src):
        f = 4 * direction + quarter
        remote(src, ring.at[f, step], ring_send.at[f, step], ring_sem.at[f, step],
               dev(0, 0, Z - 1 if direction == 0 else 1)).start()

    def toward(direction, away):
        return lax.rem(z + (Z - away if direction == 0 else away), Z)

    legs = []
    for quarter in range(4):
        first = quarter % 2
        legs += [(first, quarter, 4), (1 - first, quarter, 3)]
    for direction, quarter, far in legs:
        push(direction, quarter, 0, acc.at[rows_of(quarter, toward(direction, far))])
    for step in range(3):
        for direction, quarter, far in legs:
            if step < far - 1:
                f = 4 * direction + quarter
                arrived(ring.at[f, step], ring_sem.at[f, step])
                ring[f, step] += acc[rows_of(quarter, toward(direction, far - 1 - step)), :]
                push(direction, quarter, step + 1, ring.at[f, step])
    for quarter in range(4):
        mine = acc[rows_of(quarter, z), :]
        for direction, other, far in legs:
            if other == quarter:
                f = 4 * direction + quarter
                arrived(ring.at[f, far - 1], ring_sem.at[f, far - 1])
                mine = mine + ring[f, far - 1]
        hi, lo = split(mine)
        spread[quarter, x, :QB, :] = hi
        spread[quarter, x, QB:, :] = lo
        for d in (2, 1, 3):
            remote(spread.at[quarter, x], spread.at[quarter, x], spread_send.at[quarter],
                   spread_sem.at[quarter], dev(d, 0, 0)).start()

    for half in range(2):
        for quarter in (2 * half, 2 * half + 1):
            arrived(spread.at[quarter, pl.ds(0, 3)], spread_sem.at[quarter])
        both = None
        for k in range(X):
            lhs = jnp.concatenate([spread[2 * half, k], spread[2 * half + 1, k]], axis=0)
            term = lax.dot_general(lhs, onep[:, k * BLK:(k + 1) * BLK], NT,
                                   preferred_element_type=jnp.float32)
            both = term if both is None else both + term
        for part in range(2):
            low = 2 * QB * part
            full = both[low:low + QB] + both[low + QB:low + 2 * QB]
            for k in range(Z):
                wide[half, k, part * QB:(part + 1) * QB] = full[:, 128 * k:128 * (k + 1)]
        for d in ZORDER:
            remote(wide.at[half, lax.rem(z + d, Z)], moved.at[half, z], moved_send.at[half],
                   moved_sem.at[half], dev(0, 0, d)).start()
        moved[half, z] = wide[half, z]

    for half in range(2):
        arrived(wide.at[half, pl.ds(0, Z - 1)], moved_sem.at[half])
        flat = moved[half].reshape(HB, 128).T
        for k in range(Y):
            turned[half, k] = flat[32 * k:32 * k + 24]
        for core in (c, 1 - c):
            for d in (2, 1, 3):
                remote(turned.at[half, lax.rem(y + d, Y)], last.at[half, c * Y + y], last_send.at[half],
                       last_sem.at[half], dev(0, d, 0, core)).start()
        remote(turned.at[half, y], last.at[half, c * Y + y], last_send.at[half], last_sem.at[half],
               dev(0, 0, 0, 1 - c)).start()
        last[half, c * Y + y] = turned[half, y]

    total = None
    for half in range(2):
        arrived(last.at[half, pl.ds(0, 2 * Y - 1)], last_sem.at[half])
        for cluster in range(2):
            val = jnp.concatenate([last[half, cluster * Y + k] for k in range(Y)], axis=1)
            top = val.astype(jnp.bfloat16).astype(jnp.float32)
            lhs = jnp.concatenate([top, val - top], axis=0).astype(jnp.bfloat16)
            term = lax.dot_general(lhs, oneq[cluster, :, half * Y * HB:(half + 1) * Y * HB], NT,
                                   preferred_element_type=jnp.float32)
            total = term if total is None else total + term
    out_ref[...] = total[:SLAB] + total[24:24 + SLAB]

    for arr in range(2):
        arrived(sent.at[arr, pl.ds(0, CH * (Z - 1))], a2a_send.at[arr])
        arrived(gath.at[arr, :, pl.ds(0, 3 * GP), :], gat_send.at[arr])
    for direction, quarter, far in legs:
        f = 4 * direction + quarter
        for step in range(far):
            arrived(ring.at[f, step], ring_send.at[f, step])
    for quarter in range(4):
        arrived(spread.at[quarter, pl.ds(0, 3)], spread_send.at[quarter])
    for half in range(2):
        arrived(wide.at[half, pl.ds(0, Z - 1)], moved_send.at[half])
        arrived(last.at[half, pl.ds(0, 2 * Y - 1)], last_send.at[half])


def shards(density3, fitted_ints, virt_coeffs, dom_list):
    dma = pltpu.SemaphoreType.DMA
    flat = density3[0].reshape(ROWS * NO, NV)
    back = lax.dot_general(flat, virt_coeffs[0], NT, preferred_element_type=jnp.float32)
    half_density = back.astype(jnp.bfloat16).reshape(1, ROWS, NO, virt_coeffs.shape[1])
    metric = pl.pallas_call(
        kernel,
        out_shape=jax.ShapeDtypeStruct((SLAB, HALF), jnp.float32),
        in_specs=[pl.BlockSpec(memory_space=pl.ANY)] * 2 + [pl.BlockSpec(memory_space=pltpu.VMEM)],
        out_specs=pl.BlockSpec(memory_space=pltpu.VMEM),
        scratch_shapes=[
            pltpu.VMEM((2, 3, ROWS, 16, NV), jnp.bfloat16),
            pltpu.VMEM((2, NO, ROWS, NV), jnp.bfloat16),
            pltpu.VMEM((2, CH, BLK, NV), jnp.bfloat16),
            pltpu.VMEM((BLK, BLK), jnp.float32),
            pltpu.VMEM((8, 4, QB, BLK), jnp.float32),
            pltpu.VMEM((4, X, 2 * QB, BLK), jnp.bfloat16),
            pltpu.VMEM((2, Z, ZH, 128), jnp.float32),
            pltpu.VMEM((2, Z, ZH, 128), jnp.float32),
            pltpu.VMEM((2, Y, 24, HB), jnp.float32),
            pltpu.VMEM((2, 2 * Y, 24, HB), jnp.float32),
            pltpu.VMEM((2, 2 * X, BLK), jnp.int32),
            pltpu.VMEM((GW, DOM), jnp.bfloat16),
            pltpu.VMEM((2, HALF, DOM), jnp.bfloat16),
            dma((2, 3)), dma((2, len(PARTS))), dma((2, RELAYED, 2)), dma((2, len(PARTS))), dma((8, 4)), dma((4,)), dma((2,)), dma((2,)), dma((2,)),
            dma((2,)), dma((2,)), dma((8, 4)), dma((4,)), dma((2,)), dma((2,)),
        ],
        compiler_params=pltpu.CompilerParams(
            collective_id=0, has_side_effects=True, vmem_limit_bytes=56 * 2**20),
    )(density3[0], fitted_ints[0], dom_list)
    return (half_density, metric)


def solution(mesh):
    in_specs = (
        P("clus", "aux", None, None),
        P("clus", "aux", None, None),
        P("clus", None, None),
        P("clus", None),
    )
    out_specs = (P("clus", "aux", None, None), P("aux", "clus"))
    return jax.shard_map(shards, mesh=mesh, in_specs=in_specs, out_specs=out_specs, check_vma=False)
```

```python
import jax
import jax.numpy as jnp
from jax import lax
from jax.experimental import pallas as pl
from jax.experimental.pallas import tpu as pltpu
from jax.sharding import PartitionSpec as P

MESH = pl.DeviceIdType.MESH
X, Y, Z = 4, 4, 8
ROWS = 16
NO, NV, NAO = 48, 768, 1024
CH = NO // Z
GP = Z * ROWS
BLK = X * GP
DOM = X * Y * Z * ROWS
SLAB = 20
HALF = 1280
HB = BLK // 2
ZH = HB // Z
QB = ZH // 2
PARTS = ((0, 0, 128), (0, 128, NV), (1, 0, NV), (2, 0, NV), (3, 0, 384), (3, 384, NV),
         (4, 0, 256), (4, 256, 512), (4, 512, NV), (5, 0, 256), (5, 256, 512), (5, 512, 640), (5, 640, NV))
RELAYED = 10
GW = Z * Y * 32
ZORDER = (4, 3, 5, 2, 6, 1, 7)
NT = (((1,), (1,)), ((), ()))


def split(v):
    hi = v.astype(jnp.bfloat16)
    lo = (v - hi.astype(jnp.float32)).astype(jnp.bfloat16)
    return hi, lo


def kernel(dens, fit, virt, dom_ref, half_ref, out_ref,
           stage, orbs, backs, sent, gath, acc, ring, spread, wide, moved, turned, last, doms, onep, oneq,
           load_sem, half_sem, a2a_sem, near_sem, gat_sem, ring_sem, spread_sem, moved_sem, last_sem, misc_sem,
           a2a_send, gat_send, ring_send, spread_send, moved_send, last_send):
    c = lax.axis_index("clus")
    aux = lax.axis_index("aux")
    y = lax.rem(aux, Y)
    z = lax.rem(aux // Y, Z)
    x = aux // (Y * Z)

    def dev(dx, dy, dz, core=c):
        xx, yy, zz = lax.rem(x + dx, X), lax.rem(y + dy, Y), lax.rem(z + dz, Z)
        return (core, (xx * Z + zz) * Y + yy)

    def remote(src, dst, send, recv, where):
        return pltpu.make_async_remote_copy(
            src_ref=src, dst_ref=dst, send_sem=send, recv_sem=recv,
            device_id=where, device_id_type=MESH)

    def arrived(like, sem):
        pltpu.make_async_copy(like, like, sem).wait()

    loads = []
    for group in range(3):
        for arr, ref in ((0, dens), (1, fit)):
            load = pltpu.make_async_copy(
                ref.at[:, pl.ds(16 * group, 16), :], stage.at[arr, group], load_sem.at[arr, group])
            load.start()
            loads.append(load)

    orbs_load = pltpu.make_async_copy(virt, orbs, half_sem.at[3])
    orbs_load.start()

    barrier = pltpu.get_barrier_semaphore()
    peers = [dev(0, 0, d) for d in range(1, Z)] + [dev(d, 0, 0) for d in range(1, X)]
    for core in (c, 1 - c):
        peers += [dev(0, d, 0, core) for d in range(1, Y)]
    peers.append(dev(0, 0, 0, 1 - c))
    for peer in peers:
        pl.semaphore_signal(barrier, inc=1, device_id=peer, device_id_type=MESH)

    def relayout(group):
        for arr in range(2):
            loads[2 * group + arr].wait()
            block = stage[arr, group].astype(jnp.float32)
            sent[arr, pl.ds(16 * group, 16)] = jnp.swapaxes(block, 0, 1).astype(jnp.bfloat16)

    def slot(arr):
        return y if arr == 0 else x

    def scatter(n):
        chunk, low, high = PARTS[n]
        lanes = pl.ds(low, high - low)
        for arr in range(2):
            base = pl.multiple_of(slot(arr) * GP + z * ROWS, ROWS)
            target = gath.at[arr, chunk, pl.ds(base, ROWS), lanes]
            pltpu.make_async_copy(sent.at[arr, Z * chunk + z, :, lanes], target, a2a_sem.at[arr, n]).start()
            for d in ZORDER:
                other = lax.rem(z + d, Z)
                remote(sent.at[arr, Z * chunk + other, :, lanes], target,
                       a2a_send.at[arr], a2a_sem.at[arr, n], dev(0, 0, d)).start()

    def around(arr, d):
        return dev(0, d, 0) if arr == 0 else dev(d, 0, 0)

    def gather(n):
        chunk, low, high = PARTS[n]
        lanes = pl.ds(low, high - low)
        for arr in range(2):
            arrived(sent.at[arr, pl.ds(0, Z), :, lanes], a2a_sem.at[arr, n])
            base = pl.multiple_of(slot(arr) * GP, GP)
            part = gath.at[arr, chunk, pl.ds(base, GP), lanes]
            if n < RELAYED:
                for d in (1, 3):
                    remote(part, part, gat_send.at[arr], near_sem.at[arr, n, d // 2], around(arr, d)).start()
            else:
                for d in (2, 1, 3):
                    remote(part, part, gat_send.at[arr], gat_sem.at[arr, n], around(arr, d)).start()

    def relay(n):
        chunk, low, high = PARTS[n]
        lanes = pl.ds(low, high - low)
        for arr in range(2):
            for d in (1, 3):
                base = lax.rem(slot(arr) + 4 - d, 4) * GP
                arrived(gath.at[arr, chunk, pl.ds(0, GP), lanes], near_sem.at[arr, n, d // 2])
                rows = pl.ds(pl.multiple_of(base + (d // 2) * (GP // 2), GP // 2), GP // 2)
                part = gath.at[arr, chunk, rows, lanes]
                remote(part, part, gat_send.at[arr], gat_sem.at[arr, n], around(arr, d)).start()

    def multiply(first, final):
        for n in range(first, final + 1):
            chunk, low, high = PARTS[n]
            for arr in range(2):
                rest = GP if n < RELAYED else 3 * GP
                arrived(gath.at[arr, chunk, pl.ds(0, rest), pl.ds(low, high - low)], gat_sem.at[arr, n])
        low = PARTS[first][1]

        @pl.loop(0, 2)
        def _(half):
            rows = pl.ds(pl.multiple_of(half * HB, HB), HB)
            prod = lax.dot_general(gath[1, chunk, rows, low:high], gath[0, chunk, :, low:high], NT,
                                   preferred_element_type=jnp.float32)
            if first == 0:
                acc[rows, :] = prod
            else:
                acc[rows, :] += prod

    def back_transform(group):
        flat = stage[0, group].reshape(16 * ROWS, NV)
        for k in range(2):
            cols = slice(k * (NAO // 2), (k + 1) * (NAO // 2))
            back = lax.dot_general(flat, orbs[cols, :], NT, preferred_element_type=jnp.float32)
            backs[group, :, :, cols] = back.astype(jnp.bfloat16).reshape(ROWS, 16, NAO // 2)
        pltpu.make_async_copy(backs.at[group], half_ref.at[:, pl.ds(16 * group, 16), :],
                              half_sem.at[group]).start()

    def order_list():
        rows = [dom_ref[0:1, k * BLK:(k + 1) * BLK] for k in range(X)]
        digits = jnp.concatenate([v // 64 for v in rows] + [lax.rem(v, 64) for v in rows], axis=0)
        digits = digits.astype(jnp.float32).astype(jnp.bfloat16)
        moved_to = None
        for k in range(Y):
            n = lax.broadcasted_iota(jnp.int32, (128, BLK), 0) + 128 * k
            m = lax.broadcasted_iota(jnp.int32, (128, BLK), 1)
            source = lax.rem(m // ROWS, Z) * (Y * ROWS) + (m // GP) * ROWS + lax.rem(m, ROWS)
            perm = jnp.where(n == source, 1.0, 0.0).astype(jnp.bfloat16)
            term = lax.dot_general(digits[:, 128 * k:128 * (k + 1)], perm, (((1,), (0,)), ((), ())),
                                   preferred_element_type=jnp.float32)
            moved_to = term if moved_to is None else moved_to + term
        listed = (moved_to[:X] * 64.0 + moved_to[X:]).astype(jnp.int32)
        doms[c] = jnp.concatenate([listed, listed], axis=0)

    def one_hot_rows():
        @pl.loop(0, GW // 128)
        def _(b):
            row = lax.broadcasted_iota(jnp.int32, (128, BLK), 0) + b * 128
            pad = lax.rem(row, 32)
            goal = jnp.where(pad < SLAB, x * (Y * Z * SLAB) + (row // 32) * SLAB + pad, -1)
            for k in range(X):
                onep[pl.ds(pl.multiple_of(b * 128, 128), 128), k * BLK:(k + 1) * BLK] = jnp.where(
                    goal == doms[c, k:k + 1, :], 1.0, 0.0).astype(jnp.bfloat16)

    def one_hot_columns(cluster):
        @pl.loop(0, HALF // 128)
        def _(b):
            goal = lax.broadcasted_iota(jnp.int32, (128, GP), 0) + (c * HALF + b * 128)
            for k in range(DOM // GP):
                high, col, low = k // (2 * Y), (k // 2) % Y, k % 2
                names = doms[cluster, 2 * high + low:2 * high + low + 1, col * GP:(col + 1) * GP]
                oneq[cluster, pl.ds(pl.multiple_of(b * 128, 128), 128), k * GP:(k + 1) * GP] = jnp.where(
                    goal == names, 1.0, 0.0).astype(jnp.bfloat16)

    relayout(0)
    pl.semaphore_wait(barrier, len(peers))
    scatter(0)
    scatter(1)
    relayout(1)
    order_list()
    remote_dom = remote(doms.at[c], doms.at[c], misc_sem.at[0], misc_sem.at[1], dev(0, 0, 0, 1 - c))
    remote_dom.start()
    gather(0)
    scatter(2)
    relayout(2)
    gather(1)
    scatter(3)
    relay(0)
    orbs_load.wait()
    back_transform(0)
    gather(2)
    scatter(4)
    scatter(5)
    one_hot_rows()
    back_transform(1)
    relay(1)
    gather(3)
    scatter(6)
    scatter(7)
    remote_dom.wait()
    one_hot_columns(0)
    back_transform(2)
    relay(2)
    multiply(0, 1)
    gather(4)
    scatter(8)
    scatter(9)
    relay(3)
    multiply(2, 2)
    one_hot_columns(1)
    gather(5)
    scatter(10)
    relay(4)
    gather(6)
    scatter(11)
    scatter(12)
    relay(5)
    multiply(3, 3)
    gather(7)
    relay(6)
    gather(8)
    relay(7)
    gather(9)
    relay(8)
    multiply(4, 5)
    gather(10)
    gather(11)
    relay(9)
    gather(12)
    multiply(6, 8)
    multiply(9, 10)
    multiply(11, 12)

    def rows_of(quarter, d):
        return pl.ds(pl.multiple_of((quarter // 2) * HB + d * ZH + (quarter % 2) * QB, QB), QB)

    def push(direction, quarter, step, src):
        f = 4 * direction + quarter
        remote(src, ring.at[f, step], ring_send.at[f], ring_sem.at[f, step],
               dev(0, 0, Z - 1 if direction == 0 else 1)).start()

    def toward(direction, away):
        return lax.rem(z + (Z - away if direction == 0 else away), Z)

    legs = []
    for quarter in range(4):
        first = quarter % 2
        legs += [(first, quarter, 4), (1 - first, quarter, 3)]
    for direction, quarter, far in legs:
        push(direction, quarter, 0, acc.at[rows_of(quarter, toward(direction, far))])
    for step in range(3):
        for direction, quarter, far in legs:
            if step < far - 1:
                f = 4 * direction + quarter
                arrived(ring.at[f, step], ring_sem.at[f, step])
                ring[f, step] += acc[rows_of(quarter, toward(direction, far - 1 - step)), :]
                push(direction, quarter, step + 1, ring.at[f, step])
    for quarter in range(4):
        mine = acc[rows_of(quarter, z), :]
        for direction, other, far in legs:
            if other == quarter:
                f = 4 * direction + quarter
                arrived(ring.at[f, far - 1], ring_sem.at[f, far - 1])
                mine = mine + ring[f, far - 1]
        hi, lo = split(mine)
        spread[quarter, x, :QB, :] = hi
        spread[quarter, x, QB:, :] = lo
        for d in (2, 1, 3):
            remote(spread.at[quarter, x], spread.at[quarter, x], spread_send.at[quarter],
                   spread_sem.at[quarter], dev(d, 0, 0)).start()

    for half in range(2):
        for quarter in (2 * half, 2 * half + 1):
            arrived(spread.at[quarter, pl.ds(0, 3)], spread_sem.at[quarter])
        both = None
        for k in range(X):
            lhs = jnp.concatenate([spread[2 * half, k], spread[2 * half + 1, k]], axis=0)
            term = lax.dot_general(lhs, onep[:, k * BLK:(k + 1) * BLK], NT,
                                   preferred_element_type=jnp.float32)
            both = term if both is None else both + term
        for part in range(2):
            low = 2 * QB * part
            full = both[low:low + QB] + both[low + QB:low + 2 * QB]
            for k in range(Z):
                wide[half, k, part * QB:(part + 1) * QB] = full[:, 128 * k:128 * (k + 1)]
        for d in ZORDER:
            remote(wide.at[half, lax.rem(z + d, Z)], moved.at[half, z], moved_send.at[half],
                   moved_sem.at[half], dev(0, 0, d)).start()
        moved[half, z] = wide[half, z]

    for half in range(2):
        arrived(wide.at[half, pl.ds(0, Z - 1)], moved_sem.at[half])
        flat = moved[half].reshape(HB, 128).T
        for k in range(Y):
            turned[half, k] = flat[32 * k:32 * k + 24]
        for core in (c, 1 - c):
            for d in (2, 1, 3):
                remote(turned.at[half, lax.rem(y + d, Y)], last.at[half, c * Y + y], last_send.at[half],
                       last_sem.at[half], dev(0, d, 0, core)).start()
        remote(turned.at[half, y], last.at[half, c * Y + y], last_send.at[half], last_sem.at[half],
               dev(0, 0, 0, 1 - c)).start()
        last[half, c * Y + y] = turned[half, y]

    for group in range(3):
        arrived(backs.at[group], half_sem.at[group])
    for arr in range(2):
        arrived(sent.at[arr, pl.ds(0, CH * (Z - 1))], a2a_send.at[arr])
        arrived(gath.at[arr, :, pl.ds(0, 3 * GP), :], gat_send.at[arr])
    for direction, quarter, far in legs:
        f = 4 * direction + quarter
        arrived(ring.at[f, pl.ds(0, far)], ring_send.at[f])
    for quarter in range(4):
        arrived(spread.at[quarter, pl.ds(0, 3)], spread_send.at[quarter])
    for half in range(2):
        arrived(wide.at[half, pl.ds(0, Z - 1)], moved_send.at[half])

    total = None
    for half in range(2):
        arrived(last.at[half, pl.ds(0, 2 * Y - 1)], last_sem.at[half])
        for cluster in range(2):
            val = jnp.concatenate([last[half, cluster * Y + k] for k in range(Y)], axis=1)
            top = val.astype(jnp.bfloat16).astype(jnp.float32)
            lhs = jnp.concatenate([top, val - top], axis=0).astype(jnp.bfloat16)
            term = lax.dot_general(lhs, oneq[cluster, :, half * Y * HB:(half + 1) * Y * HB], NT,
                                   preferred_element_type=jnp.float32)
            total = term if total is None else total + term
    out_ref[...] = total[:SLAB] + total[24:24 + SLAB]

    for half in range(2):
        arrived(last.at[half, pl.ds(0, 2 * Y - 1)], last_send.at[half])


def hand_over(half_in, metric_in, half_out, metric_out, half_buf, metric_buf, sem):
    loads, stores = [], []
    for k in range(4):
        rows = pl.ds(4 * k, 4)
        loads.append(pltpu.make_async_copy(half_in.at[rows], half_buf.at[rows], sem.at[0, k]))
        stores.append(pltpu.make_async_copy(half_buf.at[rows], half_out.at[rows], sem.at[1, k]))
    loads.append(pltpu.make_async_copy(metric_in, metric_buf, sem.at[0, 4]))
    stores.append(pltpu.make_async_copy(metric_buf, metric_out, sem.at[1, 4]))
    for load in loads:
        load.start()
    for load, store in zip(loads, stores):
        load.wait()
        store.start()
    for store in stores:
        store.wait()


def shards(density3, fitted_ints, virt_coeffs, dom_list):
    dma = pltpu.SemaphoreType.DMA
    outs = (jax.ShapeDtypeStruct((ROWS, NO, NAO), jnp.bfloat16),
            jax.ShapeDtypeStruct((SLAB, HALF), jnp.float32))
    half_density, metric = pl.pallas_call(
        kernel,
        out_shape=outs,
        in_specs=[pl.BlockSpec(memory_space=pl.ANY)] * 3 + [pl.BlockSpec(memory_space=pltpu.VMEM)],
        out_specs=(pl.BlockSpec(memory_space=pl.ANY), pl.BlockSpec(memory_space=pltpu.VMEM)),
        scratch_shapes=[
            pltpu.VMEM((2, 3, ROWS, 16, NV), jnp.bfloat16),
            pltpu.VMEM((NAO, NV), jnp.bfloat16),
            pltpu.VMEM((3, ROWS, 16, NAO), jnp.bfloat16),
            pltpu.VMEM((2, NO, ROWS, NV), jnp.bfloat16),
            pltpu.VMEM((2, CH, BLK, NV), jnp.bfloat16),
            pltpu.VMEM((BLK, BLK), jnp.float32),
            pltpu.VMEM((8, 4, QB, BLK), jnp.float32),
            pltpu.VMEM((4, X, 2 * QB, BLK), jnp.bfloat16),
            pltpu.VMEM((2, Z, ZH, 128), jnp.float32),
            pltpu.VMEM((2, Z, ZH, 128), jnp.float32),
            pltpu.VMEM((2, Y, 24, HB), jnp.float32),
            pltpu.VMEM((2, 2 * Y, 24, HB), jnp.float32),
            pltpu.VMEM((2, 2 * X, BLK), jnp.int32),
            pltpu.VMEM((GW, DOM), jnp.bfloat16),
            pltpu.VMEM((2, HALF, DOM), jnp.bfloat16),
            dma((2, 3)), dma((4,)), dma((2, len(PARTS))), dma((2, RELAYED, 2)), dma((2, len(PARTS))), dma((8, 4)), dma((4,)), dma((2,)), dma((2,)), dma((2,)),
            dma((2,)), dma((2,)), dma((8,)), dma((4,)), dma((2,)), dma((2,)),
        ],
        compiler_params=pltpu.CompilerParams(
            collective_id=0, has_side_effects=True, vmem_limit_bytes=56 * 2**20),
    )(density3[0], fitted_ints[0], virt_coeffs[0], dom_list)
    half_density, metric = pl.pallas_call(
        hand_over,
        out_shape=outs,
        in_specs=[pl.BlockSpec(memory_space=pl.ANY)] * 2,
        out_specs=(pl.BlockSpec(memory_space=pl.ANY), pl.BlockSpec(memory_space=pl.ANY)),
        scratch_shapes=[pltpu.VMEM((ROWS, NO, NAO), jnp.bfloat16), pltpu.VMEM((SLAB, HALF), jnp.float32),
                        dma((2, 5))],
    )(half_density, metric)
    return (half_density[None], metric)


def solution(mesh):
    in_specs = (
        P("clus", "aux", None, None),
        P("clus", "aux", None, None),
        P("clus", None, None),
        P("clus", None),
    )
    out_specs = (P("clus", "aux", None, None), P("aux", "clus"))
    return jax.shard_map(shards, mesh=mesh, in_specs=in_specs, out_specs=out_specs, check_vma=False)
```

```python
import jax
import jax.numpy as jnp
from jax import lax
from jax.experimental import pallas as pl
from jax.experimental.pallas import tpu as pltpu
from jax.sharding import PartitionSpec as P

MESH = pl.DeviceIdType.MESH
X, Y, Z = 4, 4, 8
ROWS = 16
NO, NV, NAO = 48, 768, 1024
CH = NO // Z
GP = Z * ROWS
BLK = X * GP
DOM = X * Y * Z * ROWS
SLAB = 20
HALF = 1280
HB = BLK // 2
QB = GP // Z
PARTS = ((0, 0, 128), (0, 128, NV), (1, 0, NV), (2, 0, NV), (3, 0, 384), (3, 384, NV),
         (4, 0, 256), (4, 256, 512), (4, 512, NV), (5, 0, 256), (5, 256, 512), (5, 512, 640), (5, 640, NV))
RELAYED = 10
GW = Z * Y * 32
ZORDER = (4, 3, 5, 2, 6, 1, 7)
NT = (((1,), (1,)), ((), ()))


def split(v):
    hi = v.astype(jnp.bfloat16)
    lo = (v - hi.astype(jnp.float32)).astype(jnp.bfloat16)
    return hi, lo


def kernel(dens, fit, virt, dom_ref, half_ref, out_ref,
           stage, orbs, backs, sent, gath, acc, ring, spread, wide, moved, turned, last, doms, onep, oneq,
           load_sem, half_sem, a2a_sem, near_sem, gat_sem, ring_sem, spread_sem, moved_sem, last_sem, misc_sem,
           a2a_send, gat_send, ring_send, spread_send, moved_send, last_send):
    c = lax.axis_index("clus")
    aux = lax.axis_index("aux")
    y = lax.rem(aux, Y)
    z = lax.rem(aux // Y, Z)
    x = aux // (Y * Z)

    def dev(dx, dy, dz, core=c):
        xx, yy, zz = lax.rem(x + dx, X), lax.rem(y + dy, Y), lax.rem(z + dz, Z)
        return (core, (xx * Z + zz) * Y + yy)

    def remote(src, dst, send, recv, where):
        return pltpu.make_async_remote_copy(
            src_ref=src, dst_ref=dst, send_sem=send, recv_sem=recv,
            device_id=where, device_id_type=MESH)

    def arrived(like, sem):
        pltpu.make_async_copy(like, like, sem).wait()

    loads = []
    for group in range(3):
        for arr, ref in ((0, dens), (1, fit)):
            load = pltpu.make_async_copy(
                ref.at[:, pl.ds(16 * group, 16), :], stage.at[arr, group], load_sem.at[arr, group])
            load.start()
            loads.append(load)

    orbs_load = pltpu.make_async_copy(virt, orbs, half_sem.at[3])
    orbs_load.start()

    barrier = pltpu.get_barrier_semaphore()
    peers = [dev(0, 0, d) for d in range(1, Z)] + [dev(d, 0, 0) for d in range(1, X)]
    for core in (c, 1 - c):
        peers += [dev(0, d, 0, core) for d in range(1, Y)]
    peers.append(dev(0, 0, 0, 1 - c))
    for peer in peers:
        pl.semaphore_signal(barrier, inc=1, device_id=peer, device_id_type=MESH)

    def relayout(group):
        for arr in range(2):
            loads[2 * group + arr].wait()
            block = stage[arr, group].astype(jnp.float32)
            sent[arr, pl.ds(16 * group, 16)] = jnp.swapaxes(block, 0, 1).astype(jnp.bfloat16)

    def slot(arr):
        return y if arr == 0 else x

    def scatter(n):
        chunk, low, high = PARTS[n]
        lanes = pl.ds(low, high - low)
        for arr in range(2):
            base = pl.multiple_of(slot(arr) * GP + z * ROWS, ROWS)
            target = gath.at[arr, chunk, pl.ds(base, ROWS), lanes]
            pltpu.make_async_copy(sent.at[arr, Z * chunk + z, :, lanes], target, a2a_sem.at[arr, n]).start()
            for d in ZORDER:
                other = lax.rem(z + d, Z)
                remote(sent.at[arr, Z * chunk + other, :, lanes], target,
                       a2a_send.at[arr], a2a_sem.at[arr, n], dev(0, 0, d)).start()

    def around(arr, d):
        return dev(0, d, 0) if arr == 0 else dev(d, 0, 0)

    def gather(n):
        chunk, low, high = PARTS[n]
        lanes = pl.ds(low, high - low)
        for arr in range(2):
            arrived(sent.at[arr, pl.ds(0, Z), :, lanes], a2a_sem.at[arr, n])
            base = pl.multiple_of(slot(arr) * GP, GP)
            part = gath.at[arr, chunk, pl.ds(base, GP), lanes]
            if n < RELAYED:
                for d in (1, 3):
                    remote(part, part, gat_send.at[arr], near_sem.at[arr, n, d // 2], around(arr, d)).start()
            else:
                for d in (2, 1, 3):
                    remote(part, part, gat_send.at[arr], gat_sem.at[arr, n], around(arr, d)).start()

    def relay(n):
        chunk, low, high = PARTS[n]
        lanes = pl.ds(low, high - low)
        for arr in range(2):
            for d in (1, 3):
                base = lax.rem(slot(arr) + 4 - d, 4) * GP
                arrived(gath.at[arr, chunk, pl.ds(0, GP), lanes], near_sem.at[arr, n, d // 2])
                rows = pl.ds(pl.multiple_of(base + (d // 2) * (GP // 2), GP // 2), GP // 2)
                part = gath.at[arr, chunk, rows, lanes]
                remote(part, part, gat_send.at[arr], gat_sem.at[arr, n], around(arr, d)).start()

    def multiply(first, final, then=None, work=None):
        for n in range(first, final + 1):
            chunk, low, high = PARTS[n]
            for arr in range(2):
                rest = GP if n < RELAYED else 3 * GP
                arrived(gath.at[arr, chunk, pl.ds(0, rest), pl.ds(low, high - low)], gat_sem.at[arr, n])
        low = PARTS[first][1]

        def product(half):
            rows = pl.ds(pl.multiple_of(half * HB, HB), HB)
            prod = lax.dot_general(gath[1, chunk, rows, low:high], gath[0, chunk, :, low:high], NT,
                                   preferred_element_type=jnp.float32)
            if first == 0:
                acc[rows, :] = prod
            else:
                acc[rows, :] += prod

        if then is None:
            pl.loop(0, 2)(product)
        else:
            for half in range(2):
                product(half)
                then(work[half])

    def back_transform(group):
        flat = stage[0, group].reshape(16 * ROWS, NV)
        for k in range(2):
            cols = slice(k * (NAO // 2), (k + 1) * (NAO // 2))
            back = lax.dot_general(flat, orbs[cols, :], NT, preferred_element_type=jnp.float32)
            backs[group, :, :, cols] = back.astype(jnp.bfloat16).reshape(ROWS, 16, NAO // 2)
        pltpu.make_async_copy(backs.at[group], half_ref.at[:, pl.ds(16 * group, 16), :],
                              half_sem.at[group]).start()

    def order_list():
        rows = [dom_ref[0:1, k * BLK:(k + 1) * BLK] for k in range(X)]
        digits = jnp.concatenate([v // 64 for v in rows] + [lax.rem(v, 64) for v in rows], axis=0)
        digits = digits.astype(jnp.float32).astype(jnp.bfloat16)
        moved_to = None
        for k in range(Y):
            n = lax.broadcasted_iota(jnp.int32, (128, BLK), 0) + 128 * k
            m = lax.broadcasted_iota(jnp.int32, (128, BLK), 1)
            source = lax.rem(m // ROWS, Z) * (Y * ROWS) + (m // GP) * ROWS + lax.rem(m, ROWS)
            perm = jnp.where(n == source, 1.0, 0.0).astype(jnp.bfloat16)
            term = lax.dot_general(digits[:, 128 * k:128 * (k + 1)], perm, (((1,), (0,)), ((), ())),
                                   preferred_element_type=jnp.float32)
            moved_to = term if moved_to is None else moved_to + term
        listed = (moved_to[:X] * 64.0 + moved_to[X:]).astype(jnp.int32)
        doms[c] = jnp.concatenate([listed, listed], axis=0)

    def one_hot_rows():
        @pl.loop(0, GW // 128)
        def _(b):
            row = lax.broadcasted_iota(jnp.int32, (128, BLK), 0) + b * 128
            pad = lax.rem(row, 32)
            goal = jnp.where(pad < SLAB, x * (Y * Z * SLAB) + (row // 32) * SLAB + pad, -1)
            for k in range(X):
                onep[pl.ds(pl.multiple_of(b * 128, 128), 128), k * BLK:(k + 1) * BLK] = jnp.where(
                    goal == doms[c, k:k + 1, :], 1.0, 0.0).astype(jnp.bfloat16)

    def one_hot_columns(cluster):
        @pl.loop(0, HALF // 128)
        def _(b):
            goal = lax.broadcasted_iota(jnp.int32, (128, GP), 0) + (c * HALF + b * 128)
            for k in range(DOM // GP):
                row, col = k // Y, k % Y
                names = doms[cluster, row:row + 1, col * GP:(col + 1) * GP]
                oneq[cluster, pl.ds(pl.multiple_of(b * 128, 128), 128), k * GP:(k + 1) * GP] = jnp.where(
                    goal == names, 1.0, 0.0).astype(jnp.bfloat16)

    relayout(0)
    pl.semaphore_wait(barrier, len(peers))
    scatter(0)
    scatter(1)
    relayout(1)
    order_list()
    remote_dom = remote(doms.at[c], doms.at[c], misc_sem.at[0], misc_sem.at[1], dev(0, 0, 0, 1 - c))
    remote_dom.start()
    gather(0)
    scatter(2)
    relayout(2)
    gather(1)
    scatter(3)
    relay(0)
    orbs_load.wait()
    back_transform(0)
    gather(2)
    scatter(4)
    scatter(5)
    one_hot_rows()
    back_transform(1)
    relay(1)
    gather(3)
    scatter(6)
    scatter(7)
    remote_dom.wait()
    one_hot_columns(0)
    back_transform(2)
    relay(2)
    multiply(0, 1)
    gather(4)
    scatter(8)
    scatter(9)
    relay(3)
    multiply(2, 2)
    one_hot_columns(1)
    gather(5)
    scatter(10)
    relay(4)
    gather(6)
    scatter(11)
    scatter(12)
    relay(5)
    multiply(3, 3)
    gather(7)
    relay(6)
    gather(8)
    relay(7)
    gather(9)
    relay(8)
    multiply(4, 5)
    gather(10)
    gather(11)
    relay(9)
    gather(12)
    multiply(6, 8)
    multiply(9, 10)
    def rows_of(quarter, d):
        return pl.ds(pl.multiple_of(quarter * GP + d * QB, QB), QB)

    def push(direction, quarter, step, src):
        f = 4 * direction + quarter
        remote(src, ring.at[f, step], ring_send.at[f], ring_sem.at[f, step],
               dev(0, 0, Z - 1 if direction == 0 else 1)).start()

    def toward(direction, away):
        return lax.rem(z + (Z - away if direction == 0 else away), Z)

    legs = [(quarter % 2, quarter, 4) for quarter in range(4)]
    legs += [(1 - quarter % 2, quarter, 3) for quarter in range(4)]
    def begin(some):
        for direction, quarter, far in some:
            push(direction, quarter, 0, acc.at[rows_of(quarter, toward(direction, far))])

    multiply(11, 12, begin, (legs[:2], legs[2:]))
    for step in range(3):
        for direction, quarter, far in legs:
            if step < far - 1:
                f = 4 * direction + quarter
                arrived(ring.at[f, step], ring_sem.at[f, step])
                ring[f, step] += acc[rows_of(quarter, toward(direction, far - 1 - step)), :]
                push(direction, quarter, step + 1, ring.at[f, step])
    for quarter in range(4):
        mine = acc[rows_of(quarter, z), :]
        for direction, other, far in legs:
            if other == quarter:
                f = 4 * direction + quarter
                arrived(ring.at[f, far - 1], ring_sem.at[f, far - 1])
                mine = mine + ring[f, far - 1]
        hi, lo = split(mine)
        spread[quarter, x, :QB, :] = hi
        spread[quarter, x, QB:, :] = lo
        for d in (2, 1, 3):
            remote(spread.at[quarter, x], spread.at[quarter, x], spread_send.at[quarter],
                   spread_sem.at[quarter], dev(d, 0, 0)).start()

    for quarter in range(4):
        arrived(spread.at[quarter, pl.ds(0, 3)], spread_sem.at[quarter])
        both = None
        for k in range(X):
            term = lax.dot_general(spread[quarter, k], onep[:, k * BLK:(k + 1) * BLK], NT,
                                   preferred_element_type=jnp.float32)
            both = term if both is None else both + term
        full = both[:QB] + both[QB:]
        for k in range(Z):
            wide[quarter, k] = full[:, 128 * k:128 * (k + 1)]
        for d in ZORDER:
            remote(wide.at[quarter, lax.rem(z + d, Z)], moved.at[quarter, z], moved_send.at[quarter],
                   moved_sem.at[quarter], dev(0, 0, d)).start()
        moved[quarter, z] = wide[quarter, z]

    for quarter in range(4):
        arrived(wide.at[quarter, pl.ds(0, Z - 1)], moved_sem.at[quarter])
        flat = moved[quarter].reshape(GP, 128).T
        for k in range(Y):
            turned[quarter, k] = flat[32 * k:32 * k + 24]
        for core in (c, 1 - c):
            for d in (2, 1, 3):
                remote(turned.at[quarter, lax.rem(y + d, Y)], last.at[quarter, c * Y + y],
                       last_send.at[quarter], last_sem.at[quarter], dev(0, d, 0, core)).start()
        remote(turned.at[quarter, y], last.at[quarter, c * Y + y], last_send.at[quarter],
               last_sem.at[quarter], dev(0, 0, 0, 1 - c)).start()
        last[quarter, c * Y + y] = turned[quarter, y]

    for group in range(3):
        arrived(backs.at[group], half_sem.at[group])
    for arr in range(2):
        arrived(sent.at[arr, pl.ds(0, CH * (Z - 1))], a2a_send.at[arr])
        arrived(gath.at[arr, :, pl.ds(0, 3 * GP), :], gat_send.at[arr])
    for direction, quarter, far in legs:
        f = 4 * direction + quarter
        arrived(ring.at[f, pl.ds(0, far)], ring_send.at[f])
    for quarter in range(4):
        arrived(spread.at[quarter, pl.ds(0, 3)], spread_send.at[quarter])
        arrived(wide.at[quarter, pl.ds(0, Z - 1)], moved_send.at[quarter])

    total = None
    for quarter in range(4):
        arrived(last.at[quarter, pl.ds(0, 2 * Y - 1)], last_sem.at[quarter])
        for cluster in range(2):
            val = jnp.concatenate([last[quarter, cluster * Y + k] for k in range(Y)], axis=1)
            top = val.astype(jnp.bfloat16).astype(jnp.float32)
            lhs = jnp.concatenate([top, val - top], axis=0).astype(jnp.bfloat16)
            term = lax.dot_general(lhs, oneq[cluster, :, quarter * BLK:(quarter + 1) * BLK], NT,
                                   preferred_element_type=jnp.float32)
            total = term if total is None else total + term
    out_ref[...] = total[:SLAB] + total[24:24 + SLAB]
    for quarter in range(4):
        arrived(last.at[quarter, pl.ds(0, 2 * Y - 1)], last_send.at[quarter])


def hand_over(half_in, metric_in, half_out, metric_out, half_buf, metric_buf, sem):
    loads, stores = [], []
    for k in range(4):
        rows = pl.ds(4 * k, 4)
        loads.append(pltpu.make_async_copy(half_in.at[rows], half_buf.at[rows], sem.at[0, k]))
        stores.append(pltpu.make_async_copy(half_buf.at[rows], half_out.at[rows], sem.at[1, k]))
    loads.append(pltpu.make_async_copy(metric_in, metric_buf, sem.at[0, 4]))
    stores.append(pltpu.make_async_copy(metric_buf, metric_out, sem.at[1, 4]))
    for load in loads:
        load.start()
    for load, store in zip(loads, stores):
        load.wait()
        store.start()
    for store in stores:
        store.wait()


def shards(density3, fitted_ints, virt_coeffs, dom_list):
    dma = pltpu.SemaphoreType.DMA
    outs = (jax.ShapeDtypeStruct((ROWS, NO, NAO), jnp.bfloat16),
            jax.ShapeDtypeStruct((SLAB, HALF), jnp.float32))
    half_density, metric = pl.pallas_call(
        kernel,
        out_shape=outs,
        in_specs=[pl.BlockSpec(memory_space=pl.ANY)] * 3 + [pl.BlockSpec(memory_space=pltpu.VMEM)],
        out_specs=(pl.BlockSpec(memory_space=pl.ANY), pl.BlockSpec(memory_space=pltpu.VMEM)),
        scratch_shapes=[
            pltpu.VMEM((2, 3, ROWS, 16, NV), jnp.bfloat16),
            pltpu.VMEM((NAO, NV), jnp.bfloat16),
            pltpu.VMEM((3, ROWS, 16, NAO), jnp.bfloat16),
            pltpu.VMEM((2, NO, ROWS, NV), jnp.bfloat16),
            pltpu.VMEM((2, CH, BLK, NV), jnp.bfloat16),
            pltpu.VMEM((BLK, BLK), jnp.float32),
            pltpu.VMEM((8, 4, QB, BLK), jnp.float32),
            pltpu.VMEM((4, X, 2 * QB, BLK), jnp.bfloat16),
            pltpu.VMEM((4, Z, QB, 128), jnp.float32),
            pltpu.VMEM((4, Z, QB, 128), jnp.float32),
            pltpu.VMEM((4, Y, 24, GP), jnp.float32),
            pltpu.VMEM((4, 2 * Y, 24, GP), jnp.float32),
            pltpu.VMEM((2, 2 * X, BLK), jnp.int32),
            pltpu.VMEM((GW, DOM), jnp.bfloat16),
            pltpu.VMEM((2, HALF, DOM), jnp.bfloat16),
            dma((2, 3)), dma((4,)), dma((2, len(PARTS))), dma((2, RELAYED, 2)), dma((2, len(PARTS))),
            dma((8, 4)), dma((4,)), dma((4,)), dma((4,)), dma((2,)),
            dma((2,)), dma((2,)), dma((8,)), dma((4,)), dma((4,)), dma((4,)),
        ],
        compiler_params=pltpu.CompilerParams(
            collective_id=0, has_side_effects=True, vmem_limit_bytes=56 * 2**20),
    )(density3[0], fitted_ints[0], virt_coeffs[0], dom_list)
    half_density, metric = pl.pallas_call(
        hand_over,
        out_shape=outs,
        in_specs=[pl.BlockSpec(memory_space=pl.ANY)] * 2,
        out_specs=(pl.BlockSpec(memory_space=pl.ANY), pl.BlockSpec(memory_space=pl.ANY)),
        scratch_shapes=[pltpu.VMEM((ROWS, NO, NAO), jnp.bfloat16), pltpu.VMEM((SLAB, HALF), jnp.float32),
                        dma((2, 5))],
    )(half_density, metric)
    return (half_density[None], metric)


def solution(mesh):
    in_specs = (
        P("clus", "aux", None, None),
        P("clus", "aux", None, None),
        P("clus", None, None),
        P("clus", None),
    )
    out_specs = (P("clus", "aux", None, None), P("aux", "clus"))
    return jax.shard_map(shards, mesh=mesh, in_specs=in_specs, out_specs=out_specs, check_vma=False)
```

```python
import jax
import jax.numpy as jnp
from jax import lax
from jax.experimental import pallas as pl
from jax.experimental.pallas import tpu as pltpu
from jax.sharding import PartitionSpec as P

MESH = pl.DeviceIdType.MESH
X, Y, Z = 4, 4, 8
ROWS = 16
NO, NV, NAO = 48, 768, 1024
CH = NO // Z
GP = Z * ROWS
BLK = X * GP
DOM = X * Y * Z * ROWS
SLAB = 20
HALF = 1280
HB = BLK // 2
QB = GP // Z
PARTS = ((0, 0, 128), (0, 128, NV), (1, 0, NV), (2, 0, NV), (3, 0, 384), (3, 384, NV),
         (4, 0, 256), (4, 256, 512), (4, 512, NV), (5, 0, 256), (5, 256, 512), (5, 512, 640), (5, 640, NV))
RELAYED = 10
GW = Z * Y * 32
ZORDER = (4, 3, 5, 2, 6, 1, 7)
NT = (((1,), (1,)), ((), ()))


def split(v):
    hi = v.astype(jnp.bfloat16)
    lo = (v - hi.astype(jnp.float32)).astype(jnp.bfloat16)
    return hi, lo


def kernel(dens, fit, dom_ref, out_ref,
           stage, sent, gath, acc, ring, spread, wide, moved, turned, last, doms, onep, oneq,
           load_sem, a2a_sem, near_sem, gat_sem, ring_sem, spread_sem, moved_sem, last_sem, misc_sem,
           a2a_send, gat_send, ring_send, spread_send, moved_send, last_send):
    c = lax.axis_index("clus")
    aux = lax.axis_index("aux")
    y = lax.rem(aux, Y)
    z = lax.rem(aux // Y, Z)
    x = aux // (Y * Z)

    def dev(dx, dy, dz, core=c):
        xx, yy, zz = lax.rem(x + dx, X), lax.rem(y + dy, Y), lax.rem(z + dz, Z)
        return (core, (xx * Z + zz) * Y + yy)

    def remote(src, dst, send, recv, where):
        return pltpu.make_async_remote_copy(
            src_ref=src, dst_ref=dst, send_sem=send, recv_sem=recv,
            device_id=where, device_id_type=MESH)

    def arrived(like, sem):
        pltpu.make_async_copy(like, like, sem).wait()

    loads = []
    for group in range(3):
        for arr, ref in ((0, dens), (1, fit)):
            load = pltpu.make_async_copy(
                ref.at[:, pl.ds(16 * group, 16), :], stage.at[arr, group], load_sem.at[arr, group])
            load.start()
            loads.append(load)

    barrier = pltpu.get_barrier_semaphore()
    peers = [dev(0, 0, d) for d in range(1, Z)] + [dev(d, 0, 0) for d in range(1, X)]
    for core in (c, 1 - c):
        peers += [dev(0, d, 0, core) for d in range(1, Y)]
    peers.append(dev(0, 0, 0, 1 - c))
    for peer in peers:
        pl.semaphore_signal(barrier, inc=1, device_id=peer, device_id_type=MESH)

    def relayout(group):
        for arr in range(2):
            loads[2 * group + arr].wait()
            block = stage[arr, group].astype(jnp.float32)
            sent[arr, pl.ds(16 * group, 16)] = jnp.swapaxes(block, 0, 1).astype(jnp.bfloat16)

    def slot(arr):
        return y if arr == 0 else x

    def scatter(n):
        chunk, low, high = PARTS[n]
        lanes = pl.ds(low, high - low)
        for arr in range(2):
            base = pl.multiple_of(slot(arr) * GP + z * ROWS, ROWS)
            target = gath.at[arr, chunk, pl.ds(base, ROWS), lanes]
            pltpu.make_async_copy(sent.at[arr, Z * chunk + z, :, lanes], target, a2a_sem.at[arr, n]).start()
            for d in ZORDER:
                other = lax.rem(z + d, Z)
                remote(sent.at[arr, Z * chunk + other, :, lanes], target,
                       a2a_send.at[arr], a2a_sem.at[arr, n], dev(0, 0, d)).start()

    def around(arr, d):
        return dev(0, d, 0) if arr == 0 else dev(d, 0, 0)

    def gather(n):
        chunk, low, high = PARTS[n]
        lanes = pl.ds(low, high - low)
        for arr in range(2):
            arrived(sent.at[arr, pl.ds(0, Z), :, lanes], a2a_sem.at[arr, n])
            base = pl.multiple_of(slot(arr) * GP, GP)
            part = gath.at[arr, chunk, pl.ds(base, GP), lanes]
            if n < RELAYED:
                for d in (1, 3):
                    remote(part, part, gat_send.at[arr], near_sem.at[arr, n, d // 2], around(arr, d)).start()
            else:
                for d in (2, 1, 3):
                    remote(part, part, gat_send.at[arr], gat_sem.at[arr, n], around(arr, d)).start()

    def relay(n):
        chunk, low, high = PARTS[n]
        lanes = pl.ds(low, high - low)
        for arr in range(2):
            for d in (1, 3):
                base = lax.rem(slot(arr) + 4 - d, 4) * GP
                arrived(gath.at[arr, chunk, pl.ds(0, GP), lanes], near_sem.at[arr, n, d // 2])
                rows = pl.ds(pl.multiple_of(base + (d // 2) * (GP // 2), GP // 2), GP // 2)
                part = gath.at[arr, chunk, rows, lanes]
                remote(part, part, gat_send.at[arr], gat_sem.at[arr, n], around(arr, d)).start()

    def multiply(first, final, then=None, work=None):
        for n in range(first, final + 1):
            chunk, low, high = PARTS[n]
            for arr in range(2):
                rest = GP if n < RELAYED else 3 * GP
                arrived(gath.at[arr, chunk, pl.ds(0, rest), pl.ds(low, high - low)], gat_sem.at[arr, n])
        low = PARTS[first][1]

        def product(half):
            rows = pl.ds(pl.multiple_of(half * HB, HB), HB)
            prod = lax.dot_general(gath[1, chunk, rows, low:high], gath[0, chunk, :, low:high], NT,
                                   preferred_element_type=jnp.float32)
            if first == 0:
                acc[rows, :] = prod
            else:
                acc[rows, :] += prod

        if then is None:
            pl.loop(0, 2)(product)
        else:
            for half in range(2):
                product(half)
                then(work[half])

    def order_list():
        rows = [dom_ref[0:1, k * BLK:(k + 1) * BLK] for k in range(X)]
        digits = jnp.concatenate([v // 64 for v in rows] + [lax.rem(v, 64) for v in rows], axis=0)
        digits = digits.astype(jnp.float32).astype(jnp.bfloat16)
        moved_to = None
        for k in range(Y):
            n = lax.broadcasted_iota(jnp.int32, (128, BLK), 0) + 128 * k
            m = lax.broadcasted_iota(jnp.int32, (128, BLK), 1)
            source = lax.rem(m // ROWS, Z) * (Y * ROWS) + (m // GP) * ROWS + lax.rem(m, ROWS)
            perm = jnp.where(n == source, 1.0, 0.0).astype(jnp.bfloat16)
            term = lax.dot_general(digits[:, 128 * k:128 * (k + 1)], perm, (((1,), (0,)), ((), ())),
                                   preferred_element_type=jnp.float32)
            moved_to = term if moved_to is None else moved_to + term
        listed = (moved_to[:X] * 64.0 + moved_to[X:]).astype(jnp.int32)
        doms[c] = jnp.concatenate([listed, listed], axis=0)

    def one_hot_rows():
        @pl.loop(0, GW // 128)
        def _(b):
            row = lax.broadcasted_iota(jnp.int32, (128, BLK), 0) + b * 128
            pad = lax.rem(row, 32)
            goal = jnp.where(pad < SLAB, x * (Y * Z * SLAB) + (row // 32) * SLAB + pad, -1)
            for k in range(X):
                onep[pl.ds(pl.multiple_of(b * 128, 128), 128), k * BLK:(k + 1) * BLK] = jnp.where(
                    goal == doms[c, k:k + 1, :], 1.0, 0.0).astype(jnp.bfloat16)

    def one_hot_columns(cluster):
        @pl.loop(0, HALF // 128)
        def _(b):
            goal = lax.broadcasted_iota(jnp.int32, (128, GP), 0) + (c * HALF + b * 128)
            for k in range(DOM // GP):
                row, col = k // Y, k % Y
                names = doms[cluster, row:row + 1, col * GP:(col + 1) * GP]
                oneq[cluster, pl.ds(pl.multiple_of(b * 128, 128), 128), k * GP:(k + 1) * GP] = jnp.where(
                    goal == names, 1.0, 0.0).astype(jnp.bfloat16)

    relayout(0)
    pl.semaphore_wait(barrier, len(peers))
    scatter(0)
    scatter(1)
    relayout(1)
    order_list()
    remote_dom = remote(doms.at[c], doms.at[c], misc_sem.at[0], misc_sem.at[1], dev(0, 0, 0, 1 - c))
    remote_dom.start()
    gather(0)
    scatter(2)
    relayout(2)
    gather(1)
    scatter(3)
    relay(0)
    gather(2)
    scatter(4)
    scatter(5)
    one_hot_rows()
    relay(1)
    gather(3)
    scatter(6)
    scatter(7)
    remote_dom.wait()
    one_hot_columns(0)
    relay(2)
    multiply(0, 1)
    gather(4)
    scatter(8)
    scatter(9)
    relay(3)
    multiply(2, 2)
    one_hot_columns(1)
    gather(5)
    scatter(10)
    relay(4)
    gather(6)
    scatter(11)
    scatter(12)
    relay(5)
    multiply(3, 3)
    gather(7)
    relay(6)
    gather(8)
    relay(7)
    gather(9)
    relay(8)
    multiply(4, 5)
    gather(10)
    gather(11)
    relay(9)
    gather(12)
    multiply(6, 8)
    multiply(9, 10)
    def rows_of(quarter, d):
        return pl.ds(pl.multiple_of(quarter * GP + d * QB, QB), QB)

    def push(direction, quarter, step, src):
        f = 4 * direction + quarter
        remote(src, ring.at[f, step], ring_send.at[f], ring_sem.at[f, step],
               dev(0, 0, Z - 1 if direction == 0 else 1)).start()

    def toward(direction, away):
        return lax.rem(z + (Z - away if direction == 0 else away), Z)

    legs = [(quarter % 2, quarter, 4) for quarter in range(4)]
    legs += [(1 - quarter % 2, quarter, 3) for quarter in range(4)]
    def begin(some):
        for direction, quarter, far in some:
            push(direction, quarter, 0, acc.at[rows_of(quarter, toward(direction, far))])

    multiply(11, 12, begin, (legs[:2], legs[2:]))
    for step in range(3):
        for direction, quarter, far in legs:
            if step < far - 1:
                f = 4 * direction + quarter
                arrived(ring.at[f, step], ring_sem.at[f, step])
                ring[f, step] += acc[rows_of(quarter, toward(direction, far - 1 - step)), :]
                push(direction, quarter, step + 1, ring.at[f, step])
    for quarter in range(4):
        mine = acc[rows_of(quarter, z), :]
        for direction, other, far in legs:
            if other == quarter:
                f = 4 * direction + quarter
                arrived(ring.at[f, far - 1], ring_sem.at[f, far - 1])
                mine = mine + ring[f, far - 1]
        hi, lo = split(mine)
        spread[quarter, x, :QB, :] = hi
        spread[quarter, x, QB:, :] = lo
        for d in (2, 1, 3):
            remote(spread.at[quarter, x], spread.at[quarter, x], spread_send.at[quarter],
                   spread_sem.at[quarter], dev(d, 0, 0)).start()

    for quarter in range(4):
        arrived(spread.at[quarter, pl.ds(0, 3)], spread_sem.at[quarter])
        both = None
        for k in range(X):
            term = lax.dot_general(spread[quarter, k], onep[:, k * BLK:(k + 1) * BLK], NT,
                                   preferred_element_type=jnp.float32)
            both = term if both is None else both + term
        full = both[:QB] + both[QB:]
        for k in range(Z):
            wide[quarter, k] = full[:, 128 * k:128 * (k + 1)]
        for d in ZORDER:
            remote(wide.at[quarter, lax.rem(z + d, Z)], moved.at[quarter, z], moved_send.at[quarter],
                   moved_sem.at[quarter], dev(0, 0, d)).start()
        moved[quarter, z] = wide[quarter, z]

    for quarter in range(4):
        arrived(wide.at[quarter, pl.ds(0, Z - 1)], moved_sem.at[quarter])
        flat = moved[quarter].reshape(GP, 128).T
        for k in range(Y):
            turned[quarter, k] = flat[32 * k:32 * k + 24]
        for core in (c, 1 - c):
            for d in (2, 1, 3):
                remote(turned.at[quarter, lax.rem(y + d, Y)], last.at[quarter, c * Y + y],
                       last_send.at[quarter], last_sem.at[quarter], dev(0, d, 0, core)).start()
        remote(turned.at[quarter, y], last.at[quarter, c * Y + y], last_send.at[quarter],
               last_sem.at[quarter], dev(0, 0, 0, 1 - c)).start()
        last[quarter, c * Y + y] = turned[quarter, y]

    for arr in range(2):
        arrived(sent.at[arr, pl.ds(0, CH * (Z - 1))], a2a_send.at[arr])
        arrived(gath.at[arr, :, pl.ds(0, 3 * GP), :], gat_send.at[arr])
    for direction, quarter, far in legs:
        f = 4 * direction + quarter
        arrived(ring.at[f, pl.ds(0, far)], ring_send.at[f])
    for quarter in range(4):
        arrived(spread.at[quarter, pl.ds(0, 3)], spread_send.at[quarter])
        arrived(wide.at[quarter, pl.ds(0, Z - 1)], moved_send.at[quarter])

    total = None
    for quarter in range(4):
        arrived(last.at[quarter, pl.ds(0, 2 * Y - 1)], last_sem.at[quarter])
        for cluster in range(2):
            val = jnp.concatenate([last[quarter, cluster * Y + k] for k in range(Y)], axis=1)
            top = val.astype(jnp.bfloat16).astype(jnp.float32)
            lhs = jnp.concatenate([top, val - top], axis=0).astype(jnp.bfloat16)
            term = lax.dot_general(lhs, oneq[cluster, :, quarter * BLK:(quarter + 1) * BLK], NT,
                                   preferred_element_type=jnp.float32)
            total = term if total is None else total + term
    out_ref[...] = total[:SLAB] + total[24:24 + SLAB]
    for quarter in range(4):
        arrived(last.at[quarter, pl.ds(0, 2 * Y - 1)], last_send.at[quarter])


def hand_over(dens, orbs, metric_in, half_out, metric_out, half_buf, sem):
    stores = [pltpu.make_async_copy(metric_in, metric_out, sem.at[4])]
    stores[0].start()
    for k in range(4):
        rows = pl.ds(4 * k, 4)
        flat = dens[4 * k:4 * k + 4].reshape(4 * NO, NV)
        back = lax.dot_general(flat, orbs[...], NT, preferred_element_type=jnp.float32)
        half_buf[4 * k:4 * k + 4] = back.astype(jnp.bfloat16).reshape(4, NO, NAO)
        store = pltpu.make_async_copy(half_buf.at[rows], half_out.at[rows], sem.at[k])
        store.start()
        stores.append(store)
    for store in stores:
        store.wait()


def shards(density3, fitted_ints, virt_coeffs, dom_list):
    dma = pltpu.SemaphoreType.DMA
    outs = (jax.ShapeDtypeStruct((ROWS, NO, NAO), jnp.bfloat16),
            jax.ShapeDtypeStruct((SLAB, HALF), jnp.float32))
    metric = pl.pallas_call(
        kernel,
        out_shape=outs[1],
        in_specs=[pl.BlockSpec(memory_space=pl.ANY)] * 2 + [pl.BlockSpec(memory_space=pltpu.VMEM)],
        out_specs=pl.BlockSpec(memory_space=pltpu.VMEM),
        scratch_shapes=[
            pltpu.VMEM((2, 3, ROWS, 16, NV), jnp.bfloat16),
            pltpu.VMEM((2, NO, ROWS, NV), jnp.bfloat16),
            pltpu.VMEM((2, CH, BLK, NV), jnp.bfloat16),
            pltpu.VMEM((BLK, BLK), jnp.float32),
            pltpu.VMEM((8, 4, QB, BLK), jnp.float32),
            pltpu.VMEM((4, X, 2 * QB, BLK), jnp.bfloat16),
            pltpu.VMEM((4, Z, QB, 128), jnp.float32),
            pltpu.VMEM((4, Z, QB, 128), jnp.float32),
            pltpu.VMEM((4, Y, 24, GP), jnp.float32),
            pltpu.VMEM((4, 2 * Y, 24, GP), jnp.float32),
            pltpu.VMEM((2, 2 * X, BLK), jnp.int32),
            pltpu.VMEM((GW, DOM), jnp.bfloat16),
            pltpu.VMEM((2, HALF, DOM), jnp.bfloat16),
            dma((2, 3)), dma((2, len(PARTS))), dma((2, RELAYED, 2)), dma((2, len(PARTS))),
            dma((8, 4)), dma((4,)), dma((4,)), dma((4,)), dma((2,)),
            dma((2,)), dma((2,)), dma((8,)), dma((4,)), dma((4,)), dma((4,)),
        ],
        compiler_params=pltpu.CompilerParams(
            collective_id=0, has_side_effects=True, vmem_limit_bytes=56 * 2**20),
    )(density3[0], fitted_ints[0], dom_list)
    half_density, metric = pl.pallas_call(
        hand_over,
        out_shape=outs,
        in_specs=[pl.BlockSpec(memory_space=pltpu.VMEM)] * 3,
        out_specs=(pl.BlockSpec(memory_space=pl.ANY), pl.BlockSpec(memory_space=pl.ANY)),
        scratch_shapes=[pltpu.VMEM((ROWS, NO, NAO), jnp.bfloat16), dma((5,))],
    )(density3[0], virt_coeffs[0], metric)
    return (half_density[None], metric)


def solution(mesh):
    in_specs = (
        P("clus", "aux", None, None),
        P("clus", "aux", None, None),
        P("clus", None, None),
        P("clus", None),
    )
    out_specs = (P("clus", "aux", None, None), P("aux", "clus"))
    return jax.shard_map(shards, mesh=mesh, in_specs=in_specs, out_specs=out_specs, check_vma=False)
```
